32 devices in a mesh: inst: 4 (over z), span: 2 (over x), chord: 4 (over y, core).
Axes of the slice: x: 2, y: 2, z: 4, core: 2. Of those that a mesh axis runs over, the one named last changes fastest.
Arguments:
- adj_source: float32 [4, 8, 32, 1920], P('inst', 'span', 'chord'), may hold values from -6 to 6
- adj_start: float32 [4, 8, 32, 1920], P('inst', 'span', 'chord'), may hold values from -4 to 4
- tiles: bfloat16 [4, 8, 32, 4, 6, 1920], P('inst', 'span', 'chord'), may hold values from -1.25 to 1.25
- tile_cols: int32 [8, 32, 4], P('span', 'chord'), may hold values from 0 to 8, as said below
- inverse_diag: bfloat16 [4, 8, 32, 6, 1920], P('inst', 'span', 'chord'), as said below
- face_src: int32 [2, 2048], P(None, ('span', 'chord')), may hold values from 0 to 10239, as said below
- face_dst: int32 [2, 2048], P(None, ('span', 'chord')), may hold values from 0 to 10239, as said below
- lag_coef: bfloat16 [4, 72, 2048], P('inst', None, ('span', 'chord')), may hold values from -2.5 to 2.5
Outputs:
- adjoint: float32 [4, 8, 32, 1920], P('inst', 'span', 'chord')
- residual: float32 [4, 8, 32, 1920], P('inst', 'span', 'chord')
The draws below stay inside these ranges and needn't reach their ends.
Inputs may be any that keep to these rules, and one draw needn't show every extreme that they name: `tile_cols`: each block row names code 4 (its own block) once and three distinct other codes; code 3 a + b means the block a - 1 spanwise and b - 1 chordwise away. `face_src`: for each side, the 256 entries of one span and chord group are distinct cell numbers of that group. `face_dst`: for each side, the 256 entries of one span and chord group are distinct cell numbers of that group. `inverse_diag`: diagonal entries of each 6 x 6 block lie in 0.4 to 1.6, off-diagonal entries in -0.35 to 0.35.
All inputs are finite; a program needn't handle non-finite values.
Results may differ from the reference program's by a relative error of at most 0.0003.
Values sent between devices are 32-bit elements; how exact they have to be, the bound alone decides.
A program may use at most 64 MiB of HBM per device.

```python
import math
import jax
import jax.numpy as jnp
from jax import lax

NV = 6
BLK = 320
K = 4
SB = 4
CB = 8
PF = 256
SWEEPS = 2
NT = 4
LAG = 1
NSB = 8
NCB = 32
CELLS_DEV = 10240
FACES = 2048
N_SPAN = 2
N_CHORD = 4


def draw_inverse_diag(key, part):
    first, second = jax.random.split(key)
    shape = (NT, NSB, NCB, NV, NV, BLK)
    diagonal = jax.random.uniform(first, shape, jnp.float32, 0.5, 1.5)
    coupling = jnp.clip(0.2 * jax.random.normal(second, shape, jnp.float32), -0.35, 0.35)
    same = (jnp.arange(NV)[:, None] == jnp.arange(NV)[None, :])[:, :, None]
    return jnp.where(same, diagonal, coupling).reshape(NT, NSB, NCB, NV, NV * BLK).astype(jnp.bfloat16)


def draw_tile_cols(key, part):
    others = jnp.array([0, 1, 2, 3, 5, 6, 7, 8], dtype=jnp.int32)

    def one_row(row_key):
        pick_key, order_key = jax.random.split(row_key)
        chosen = jax.random.permutation(pick_key, others)[:3]
        slots = jnp.concatenate([chosen, jnp.array([4], dtype=jnp.int32)])
        return jax.random.permutation(order_key, slots)
    return jax.vmap(one_row)(jax.random.split(key, NSB * NCB)).reshape(NSB, NCB, K).astype(jnp.int32)


def face_draw(key):
    groups = FACES // PF

    def one_list(list_key):
        pick_key, order_key = jax.random.split(list_key)
        middle = (jax.random.permutation(pick_key, CELLS_DEV - 2)[:PF - 2] + 1).astype(jnp.int32)
        ends = jnp.array([0, CELLS_DEV - 1], dtype=jnp.int32)
        return jax.random.permutation(order_key, jnp.concatenate([ends, middle])).astype(jnp.int32)
    return jax.vmap(one_list)(jax.random.split(key, 2 * groups)).reshape(2, FACES)


def draw_face_src(key, part):
    return face_draw(jax.random.fold_in(key, 11))


def draw_face_dst(key, part):
    return face_draw(jax.random.fold_in(key, 23))


def levels(stream_key, shape, pieces, low, largest):
    level, own = 1.0, jax.random.fold_in(stream_key, 6)
    for axis_at, shards_of in pieces:
        steps = jnp.exp(jax.random.uniform(jax.random.fold_in(own, axis_at), (shards_of,), jnp.float32, low / len(pieces), largest / len(pieces)))
        level = level * jnp.repeat(steps, shape[axis_at] // shards_of).reshape([-1 if axis == axis_at else 1 for axis in range(len(shape))])
    return level


def centred(rng, dims, scale, reach, cuts=(), held_as=jnp.bfloat16):
    result = scale * jax.random.normal(rng, dims, jnp.float32)
    if cuts:
        result = result * levels(rng, dims, cuts, -0.22, 0.18)
    return jnp.clip(result, -reach, reach).astype(held_as)


def setup_inputs(seed: int = 0) -> dict:
    splits = jax.random.split(jax.random.key(seed), 9)
    adj_source = centred(splits[0], (NT, NSB, NCB, NV * BLK), 1.0, 6.0, ((0, 4), (1, 2), (2, 4)), jnp.float32)
    adj_start = centred(splits[1], (NT, NSB, NCB, NV * BLK), 0.5, 4.0, ((0, 4), (1, 2), (2, 4)), jnp.float32)
    tiles = centred(splits[2], (NT, NSB, NCB, K, NV, NV * BLK), (K * NV) ** -0.5, 1.25, ((0, 4), (1, 2), (2, 4)))
    tile_cols = draw_tile_cols(jax.random.fold_in(splits[8], 71), 0)
    inverse_diag = draw_inverse_diag(jax.random.fold_in(splits[8], 71), 0)
    face_src = draw_face_src(jax.random.fold_in(splits[8], 71), 0)
    face_dst = draw_face_dst(jax.random.fold_in(splits[8], 71), 0)
    lag_coef = centred(splits[7], (NT, 2 * NV * NV, FACES), NV ** -0.5, 2.5, ((0, 4), (2, 8)))
    return dict(adj_source=adj_source, adj_start=adj_start, tiles=tiles, tile_cols=tile_cols, inverse_diag=inverse_diag, face_src=face_src, face_dst=face_dst, lag_coef=lag_coef)


rotor_rate = 0.25
spectral_viscosity = 0.03
highest = lax.Precision.HIGHEST


def spectral_row(instance, total):
    others = jnp.arange(total, dtype=jnp.int32)
    offset = jnp.mod(others - instance, total)
    angle = (math.pi / total) * offset.astype(jnp.float32)
    parity = jnp.where(jnp.mod(offset, 2) == 0, 1.0, -1.0).astype(jnp.float32)
    sine = jnp.where(offset == 0, 1.0, jnp.sin(angle)).astype(jnp.float32)
    first = jnp.where(offset == 0, 0.0, 0.5 * parity * jnp.cos(angle) / sine)
    second = jnp.where(offset == 0, -(total * total + 2) / 12.0, -0.5 * parity / (sine * sine))
    return (rotor_rate * first - spectral_viscosity * second).astype(jnp.float32)


def extend(state):
    wrapped = jnp.concatenate([state[:, -1:], state, state[:, :1]], axis=1)
    return jnp.pad(wrapped, ((1, 1), (0, 0), (0, 0)))


def tile_product(extended, tiles, tile_cols):
    rows = tile_cols.shape[0]
    cols = tile_cols.shape[1]
    width = extended.shape[-1]
    selected = jnp.zeros((rows, cols, tile_cols.shape[2], width), jnp.float32)
    for code in range(9):
        view = extended[code // 3: code // 3 + rows, code % 3: code % 3 + cols]
        selected = selected + jnp.where((tile_cols == code)[..., None], view[:, :, None, :], 0.0)
    cells = width // NV
    coupled = tiles.astype(jnp.float32).reshape(rows, cols, tile_cols.shape[2], NV, NV, cells) * selected.reshape(rows, cols, tile_cols.shape[2], 1, NV, cells)
    return jnp.sum(coupled, axis=(2, 4)).reshape(rows, cols, width)


def lag_pack(blocks, faces):
    return blocks[faces // BLK, :, faces % BLK].T


def lag_apply(pack_behind, pack_ahead, coef, dst_behind, dst_ahead):
    coupling = coef.astype(jnp.float32).reshape(2, NV, NV, PF)
    term = jnp.zeros((SB * CB, NV, BLK), jnp.float32)
    for direction, packed, target in ((0, pack_behind, dst_behind), (1, pack_ahead, dst_ahead)):
        contrib = jnp.sum(coupling[direction] * packed[None, :, :], axis=1)
        term = term.at[target // BLK, :, target % BLK].add(contrib.T)
    return term


def precondition(inverse, residual):
    lead = residual.shape[:-1]
    product = inverse.astype(jnp.float32).reshape(lead + (NV, NV, BLK)) * residual.reshape(lead + (1, NV, BLK))
    return jnp.sum(product, axis=-2).reshape(lead + (NV * BLK,))


def reference(adj_source, adj_start, tiles, tile_cols, inverse_diag, face_src, face_dst, lag_coef):
    groups = N_SPAN * N_CHORD

    def grouped(state):
        return state.reshape(N_SPAN, SB, N_CHORD, CB, NV, BLK).transpose(0, 2, 1, 3, 4, 5).reshape(groups, SB * CB, NV, BLK)

    def ungrouped(blocks):
        return blocks.reshape(N_SPAN, N_CHORD, SB, CB, NV * BLK).transpose(0, 2, 1, 3, 4).reshape(NSB, NCB, NV * BLK)

    src_groups = face_src.reshape(2, groups, PF)
    dst_groups = face_dst.reshape(2, groups, PF)

    def apply_operator(state):
        def one_instance(instance):
            own = state[instance]
            tile_term = tile_product(extend(own), tiles[instance], tile_cols)
            weights = spectral_row(instance, NT)
            spectral_term = jnp.einsum('s,spqf->pqf', weights, state, precision=highest)
            behind = grouped(state[jnp.mod(instance - LAG, NT)])
            ahead = grouped(state[jnp.mod(instance + LAG, NT)])
            pack_behind = jax.vmap(lag_pack)(behind, src_groups[0])
            pack_ahead = jax.vmap(lag_pack)(ahead, src_groups[1])
            coef_groups = lag_coef[instance].reshape(2 * NV * NV, groups, PF).transpose(1, 0, 2)
            lag_term = jax.vmap(lag_apply)(pack_behind, pack_ahead, coef_groups, dst_groups[0], dst_groups[1])
            return tile_term + spectral_term + ungrouped(lag_term)

        return lax.map(one_instance, jnp.arange(NT, dtype=jnp.int32))

    def update_one(pair):
        return precondition(pair[0], pair[1])

    state = adj_start
    residual = adj_source
    for sweep_index in range(SWEEPS):
        residual = adj_source - apply_operator(state)
        state = state + lax.map(update_one, (inverse_diag, residual))
    return state, residual
```

```python
import math

import jax
import jax.numpy as jnp
from jax import lax
from jax.experimental import pallas as pl
from jax.experimental.pallas import tpu as pltpu
from jax.sharding import PartitionSpec as P

NV = 6
SWEEPS = 2
BLADES = 4
RIGHT, LEFT = 0, 1

rotor_rate = 0.25
spectral_viscosity = 0.03
MESH = pl.DeviceIdType.MESH


def spectral_weight(offset, total):
    m = offset % total
    if m == 0:
        return spectral_viscosity * (total * total + 2) / 12.0
    parity = -1.0 if m % 2 else 1.0
    angle = math.pi * m / total
    first = 0.5 * parity * math.cos(angle) / math.sin(angle)
    second = -0.5 * parity / math.sin(angle) ** 2
    return rotor_rate * first - spectral_viscosity * second


def split3(x):
    high = x.astype(jnp.bfloat16)
    rest = x - high.astype(jnp.float32)
    middle = rest.astype(jnp.bfloat16)
    low = (rest - middle.astype(jnp.float32)).astype(jnp.bfloat16)
    return jnp.concatenate([high, middle, low], axis=0)


def sum3(y):
    n = y.shape[0] // 3
    return (y[2 * n :] + y[n : 2 * n]) + y[:n]


def make_kernel(sizes, n_inst, n_span, n_chord):
    SB, CB, W, K, PF = sizes
    BLK = W // NV
    PAIR = 2 * BLK
    NP = NV // 2
    BLKS = SB * CB
    EXT = CB + 2
    half = n_inst // 2
    lag = n_inst // BLADES

    def kernel(
        x0_ref, source_ref, cols_ref, fsrc_ref, fdst_ref, coef_ref, tiles_hbm, inv_hbm,
        adj_ref, res_ref,
        tiles_ref, inv_ref, x1_ref, xb_ref, base_ref, g_ref, coef32_ref, oh_src, oh_dst, mask_src, mask_dst,
        gat_ref, sum_ref, col_send, corn_send, col_recv, row_recv, corn_recv, pack_send, pack_recv,
        load_sem, gs_sem, gr_sem, hs_sem, hr_sem, ps_sem, pr_sem,
    ):
        t = lax.axis_index("inst")
        sp = lax.axis_index("span")
        ch = lax.axis_index("chord")
        ch_up = lax.rem(ch + 1, n_chord)
        ch_dn = lax.rem(ch + n_chord - 1, n_chord)
        t_up = lax.rem(t + lag, n_inst)
        t_dn = lax.rem(t + n_inst - lag, n_inst)
        has_lo = sp > 0
        has_hi = sp < n_span - 1

        loads = []
        for p in range(SB):
            loads.append(
                pltpu.make_async_copy(
                    tiles_hbm.at[pl.ds(p * CB, CB)], tiles_ref.at[pl.ds(p * CB, CB)], load_sem.at[p]
                )
            )
        inv_load = pltpu.make_async_copy(inv_hbm, inv_ref, load_sem.at[SB])
        for load in loads:
            load.start()
        inv_load.start()

        barrier = pltpu.get_barrier_semaphore()

        def greet(i, s, c):
            pl.semaphore_signal(barrier, inc=1, device_id=(i, s, c), device_id_type=MESH)

        count = 4 + 3 * jnp.where(has_lo, 1, 0) + 3 * jnp.where(has_hi, 1, 0)
        greet(t_up, sp, ch)
        greet(t_dn, sp, ch)
        greet(t, sp, ch_up)
        greet(t, sp, ch_dn)
        if lag != 1:
            count = count + jnp.where(t > 0, 1, 0) + jnp.where(t < n_inst - 1, 1, 0)

            @pl.when(t > 0)
            def _():
                greet(t - 1, sp, ch)

            @pl.when(t < n_inst - 1)
            def _():
                greet(t + 1, sp, ch)

        @pl.when(has_lo)
        def _():
            for c in (ch, ch_up, ch_dn):
                greet(t, sp - 1, c)

        @pl.when(has_hi)
        def _():
            for c in (ch, ch_up, ch_dn):
                greet(t, sp + 1, c)

        pl.semaphore_wait(barrier, count)

        def at(direction):
            return t if direction == RIGHT else n_inst - 1 - t

        def stream(sweep, direction, j, p, src):
            target = t + 1 if direction == RIGHT else t - 1
            return pltpu.make_async_remote_copy(
                src_ref=src,
                dst_ref=gat_ref.at[sweep, direction, j, p],
                send_sem=gs_sem.at[sweep, direction, j, p],
                recv_sem=gr_sem.at[sweep, direction, j, p],
                device_id=(target, sp, ch),
                device_id_type=MESH,
            )

        def weight(direction, hops):
            return spectral_weight(-hops if direction == RIGHT else hops, n_inst)

        def send_own(sweep, p, x_ref):
            for d in (RIGHT, LEFT):

                @pl.when(at(d) < half)
                def _():
                    stream(sweep, d, 0, p, x_ref.at[p]).start()

        def forward(sweep, p):
            for d in (RIGHT, LEFT):
                for j in range(1, half):

                    @pl.when(jnp.logical_and(at(d) >= j, at(d) < half))
                    def _():
                        got = gat_ref.at[sweep, d, j - 1, p]
                        stream(sweep, d, j - 1, p, got).wait_recv()
                        stream(sweep, d, j, p, got).start()

        def collect(sweep, p, x_ref):
            for d in (RIGHT, LEFT):

                @pl.when(at(d) == half)
                def _():
                    for j in range(half):
                        stream(sweep, d, j, p, gat_ref.at[sweep, d, j, p]).wait_recv()
                    for j in range(n_inst - 1 - half):
                        total = weight(d, 1 + j) * x_ref[p]
                        for i in range(half):
                            total = total + weight(d, 2 + j + i) * gat_ref[sweep, d, i, p]
                        sum_ref[sweep, d, j, p] = total
                        stream(sweep, d, j, p, sum_ref.at[sweep, d, j, p]).start()

                for place in range(half + 1, n_inst):

                    @pl.when(at(d) == place)
                    def _():
                        for j in range(n_inst - place):
                            stream(sweep, d, j, p, gat_ref.at[sweep, d, j, p]).wait_recv()
                        for j in range(n_inst - 1 - place):
                            sum_ref[sweep, d, j, p] = gat_ref[sweep, d, j + 1, p] + weight(d, 1 + j) * x_ref[p]
                            stream(sweep, d, j, p, sum_ref.at[sweep, d, j, p]).start()

        def spectral(sweep, p, x_ref):
            res_ref[p] = base_ref[p] - spectral_weight(0, n_inst) * x_ref[p]
            for d in (RIGHT, LEFT):
                for i in range(half):

                    @pl.when(jnp.logical_and(at(d) > i, at(d) <= half))
                    def _():
                        res_ref[p] = res_ref[p] - weight(d, 1 + i) * gat_ref[sweep, d, i, p]

                @pl.when(at(d) > half)
                def _():
                    res_ref[p] = res_ref[p] - gat_ref[sweep, d, 0, p]

        def drain(sweep, p):
            for d in (RIGHT, LEFT):
                for j in range(half):
                    raw = jnp.logical_and(at(d) < half, at(d) >= j)
                    summed = jnp.logical_and(at(d) >= half, at(d) < n_inst - 1 - j)

                    @pl.when(jnp.logical_or(raw, summed))
                    def _():
                        stream(sweep, d, j, p, gat_ref.at[sweep, d, j, p]).wait_send()

        def halo(sweep, place, src, dst, device):
            return pltpu.make_async_remote_copy(
                src_ref=src,
                dst_ref=dst,
                send_sem=hs_sem.at[sweep, place],
                recv_sem=hr_sem.at[sweep, place],
                device_id=device,
                device_id_type=MESH,
            )

        def columns(sweep):
            return [
                halo(sweep, 0, col_send.at[sweep, 0], col_recv.at[sweep, 0], (t, sp, ch_up)),
                halo(sweep, 1, col_send.at[sweep, 1], col_recv.at[sweep, 1], (t, sp, ch_dn)),
            ]

        def upward(sweep, x_ref):
            return [
                halo(sweep, 2, x_ref.at[SB - 1], row_recv.at[sweep, 0], (t, sp + 1, ch)),
                halo(sweep, 4, corn_send.at[sweep, 0], corn_recv.at[sweep, 0], (t, sp + 1, ch_up)),
                halo(sweep, 5, corn_send.at[sweep, 1], corn_recv.at[sweep, 1], (t, sp + 1, ch_dn)),
            ]

        def downward(sweep, x_ref):
            return [
                halo(sweep, 3, x_ref.at[0], row_recv.at[sweep, 1], (t, sp - 1, ch)),
                halo(sweep, 6, corn_send.at[sweep, 2], corn_recv.at[sweep, 2], (t, sp - 1, ch_up)),
                halo(sweep, 7, corn_send.at[sweep, 3], corn_recv.at[sweep, 3], (t, sp - 1, ch_dn)),
            ]

        def send_halos(sweep, x_ref):
            for p in range(SB):
                col_send[sweep, 0, p : p + 1, :] = x_ref[p, CB - 1 : CB, :]
                col_send[sweep, 1, p : p + 1, :] = x_ref[p, 0:1, :]
            corn_send[sweep, 0] = x_ref[SB - 1, CB - 1 : CB, :]
            corn_send[sweep, 1] = x_ref[SB - 1, 0:1, :]
            corn_send[sweep, 2] = x_ref[0, CB - 1 : CB, :]
            corn_send[sweep, 3] = x_ref[0, 0:1, :]
            for copy in columns(sweep):
                copy.start()

            @pl.when(has_hi)
            def _():
                for copy in upward(sweep, x_ref):
                    copy.start()

            @pl.when(has_lo)
            def _():
                for copy in downward(sweep, x_ref):
                    copy.start()

        def put(row, value):
            xb_ref[row] = jnp.broadcast_to(value, (8, W))

        def take_halos(sweep, x_ref):
            for copy in columns(sweep):
                copy.wait_recv()
            for p in range(SB):
                put((p + 1) * EXT, col_recv[sweep, 0, p : p + 1, :])
                put((p + 1) * EXT + CB + 1, col_recv[sweep, 1, p : p + 1, :])

            @pl.when(has_lo)
            def _():
                for copy in upward(sweep, x_ref):
                    copy.wait_recv()
                for q in range(CB):
                    put(q + 1, row_recv[sweep, 0, q : q + 1, :])
                put(0, corn_recv[sweep, 0])
                put(CB + 1, corn_recv[sweep, 1])

            @pl.when(has_hi)
            def _():
                for copy in downward(sweep, x_ref):
                    copy.wait_recv()
                top = (SB + 1) * EXT
                for q in range(CB):
                    put(top + q + 1, row_recv[sweep, 1, q : q + 1, :])
                put(top, corn_recv[sweep, 2])
                put(top + CB + 1, corn_recv[sweep, 3])

        def drain_halos(sweep, x_ref):
            for copy in columns(sweep):
                copy.wait_send()

            @pl.when(has_hi)
            def _():
                for copy in upward(sweep, x_ref):
                    copy.wait_send()

            @pl.when(has_lo)
            def _():
                for copy in downward(sweep, x_ref):
                    copy.wait_send()

        def put_own(p, x_ref):
            for q in range(CB):
                put((p + 1) * EXT + q + 1, x_ref[p, q : q + 1, :])

        def face_tables(faces_ref, onehot, mask):
            faces = jnp.concatenate([faces_ref[s : s + 1, :] for s in (0, 0, 1, 1)], axis=1)
            block = ((faces.astype(jnp.float32) + 0.5) * (1.0 / BLK)).astype(jnp.int32)
            parity = lax.rem(lax.broadcasted_iota(jnp.int32, (1, 4 * PF), 1), 2 * PF) >= PF
            cell = faces - block * BLK + jnp.where(parity, BLK, 0)
            rows = lax.broadcasted_iota(jnp.int32, (BLKS, 4 * PF), 0)
            mask[...] = jnp.where(rows == block, 1.0, 0.0)
            step = 128

            def fill(i, _):
                first = pl.multiple_of(i * step, step)
                lanes = lax.broadcasted_iota(jnp.int32, (step, 4 * PF), 0) + first
                onehot[pl.ds(first, step), :] = jnp.where(lanes == cell, 1.0, 0.0).astype(jnp.bfloat16)
                return 0

            lax.fori_loop(0, PAIR // step, fill, 0)

        def packs(sweep):
            return [
                pltpu.make_async_remote_copy(
                    src_ref=pack_send.at[sweep, side],
                    dst_ref=pack_recv.at[sweep, side],
                    send_sem=ps_sem.at[sweep, side],
                    recv_sem=pr_sem.at[sweep, side],
                    device_id=(target, sp, ch),
                    device_id_type=MESH,
                )
                for side, target in ((0, t_up), (1, t_dn))
            ]

        def send_packs(sweep, x_ref):
            pairs = [x_ref[:, :, m * PAIR : (m + 1) * PAIR].reshape(BLKS, PAIR) for m in range(NP)]
            picked = sum3(
                jnp.dot(
                    split3(jnp.concatenate(pairs, axis=0)), oh_src[...], preferred_element_type=jnp.float32
                )
            )
            for m in range(NP):
                row = jnp.sum(picked[m * BLKS : (m + 1) * BLKS] * mask_src[...], axis=0, keepdims=True)
                for side in (0, 1):
                    pack_send[sweep, side, m : m + 1, :] = row[:, side * 2 * PF : (side + 1) * 2 * PF]
            for copy in packs(sweep):
                copy.start()

        def take_packs(sweep):
            for copy in packs(sweep):
                copy.wait_recv()
            contrib = []
            for side in (0, 1):
                total = jnp.zeros((NV, PF), jnp.float32)
                for w in range(NV):
                    rows = pl.ds(side * NV * NV + w, NV, stride=NV)
                    coupling = jnp.concatenate([coef32_ref[c, rows, :] for c in range(PF // 128)], axis=1)
                    first = (w % 2) * PF
                    total = total + coupling * pack_recv[sweep, side, w // 2 : w // 2 + 1, first : first + PF]
                contrib.append(total)
            spread = []
            for m in range(NP):
                row = jnp.concatenate(
                    [contrib[s][2 * m + odd : 2 * m + odd + 1, :] for s in (0, 1) for odd in (0, 1)], axis=1
                )
                spread.append(mask_dst[...] * row)
            term = sum3(
                lax.dot_general(
                    split3(jnp.concatenate(spread, axis=0)),
                    oh_dst[...],
                    (((1,), (1,)), ((), ())),
                    preferred_element_type=jnp.float32,
                )
            )
            for m in range(NP):
                lanes = slice(m * PAIR, (m + 1) * PAIR)
                base_ref[:, :, lanes] = base_ref[:, :, lanes] - term[m * BLKS : (m + 1) * BLKS].reshape(
                    SB, CB, PAIR
                )

        def keep(slot, q, product):
            folded = product[:, :PAIR]
            for m in range(1, NP):
                folded = folded + product[:, m * PAIR : (m + 1) * PAIR]
            for c in range(PAIR // 128):
                g_ref[slot, c, q * 8 : q * 8 + NV, :] = folded[:, c * 128 : (c + 1) * 128]

        def variable(slot, v):
            rows = pl.ds(v, CB, stride=8)
            return jnp.concatenate([g_ref[slot, c, rows, :] for c in range(PAIR // 128)], axis=1)

        def flat(slot):
            low = lax.broadcasted_iota(jnp.int32, (CB, PAIR), 1) < BLK
            parts = []
            for m in range(NP):
                even = variable(slot, 2 * m)
                odd = variable(slot, 2 * m + 1)
                parts.append(
                    jnp.where(low, even, odd) + pltpu.roll(jnp.where(low, odd, even), BLK, axis=1)
                )
            return parts

        def tile_row(p):
            for q in range(CB):
                block = p * CB + q
                total = None
                for k in range(K):
                    code = cols_ref[block * K + k]
                    up = jnp.where(code >= 6, 2, jnp.where(code >= 3, 1, 0))
                    row = (p + up) * EXT + q + code - 3 * up
                    part = tiles_ref[block, k].astype(jnp.float32) * xb_ref[row, 0:NV, :]
                    total = part if total is None else total + part
                keep(0, q, total)
            for m, part in enumerate(flat(0)):
                lanes = slice(m * PAIR, (m + 1) * PAIR)
                base_ref[p, :, lanes] = source_ref[p, :, lanes] - part

        def update_row(p, x_ref, out_ref):
            for q in range(CB):
                keep(1, q, inv_ref[p * CB + q].astype(jnp.float32) * res_ref[p, q : q + 1, :])
            for m, part in enumerate(flat(1)):
                lanes = slice(m * PAIR, (m + 1) * PAIR)
                out_ref[p, :, lanes] = x_ref[p, :, lanes] + part

        def loop(body):
            def step(p, _):
                body(p)
                return 0

            lax.fori_loop(0, SB, step, 0)

        send_halos(0, x0_ref)
        loop(lambda p: send_own(0, p, x0_ref))

        @pl.when(jnp.logical_not(has_lo))
        def _():
            for q in range(EXT):
                xb_ref[q] = jnp.zeros((8, W), jnp.float32)

        @pl.when(jnp.logical_not(has_hi))
        def _():
            for q in range(EXT):
                xb_ref[(SB + 1) * EXT + q] = jnp.zeros((8, W), jnp.float32)

        face_tables(fsrc_ref, oh_src, mask_src)
        send_packs(0, x0_ref)
        loop(lambda p: put_own(p, x0_ref))
        face_tables(fdst_ref, oh_dst, mask_dst)
        for c in range(PF // 128):
            coef32_ref[c] = coef_ref[:, c * 128 : (c + 1) * 128].astype(jnp.float32)
        for load in loads:
            load.wait()
        inv_load.wait()
        take_halos(0, x0_ref)

        def first_tiles(p):
            tile_row(p)
            forward(0, p)

        loop(first_tiles)
        take_packs(0)

        def first_update(p):
            collect(0, p, x0_ref)
            spectral(0, p, x0_ref)
            update_row(p, x0_ref, x1_ref)
            send_own(1, p, x1_ref)
            put_own(p, x1_ref)

        loop(first_update)

        send_halos(1, x1_ref)
        send_packs(1, x1_ref)
        take_halos(1, x1_ref)

        def last_tiles(p):
            tile_row(p)
            forward(1, p)

        loop(last_tiles)
        take_packs(1)

        def last_update(p):
            collect(1, p, x1_ref)
            spectral(1, p, x1_ref)
            update_row(p, x1_ref, adj_ref)

        loop(last_update)

        for sweep, x_ref in ((0, x0_ref), (1, x1_ref)):
            loop(lambda p: drain(sweep, p))
            drain_halos(sweep, x_ref)
            for copy in packs(sweep):
                copy.wait_send()

    scratch = [
        pltpu.VMEM((BLKS, K, NV, W), jnp.bfloat16),
        pltpu.VMEM((BLKS, NV, W), jnp.bfloat16),
        pltpu.VMEM((SB, CB, W), jnp.float32),
        pltpu.VMEM(((SB + 2) * EXT, 8, W), jnp.float32),
        pltpu.VMEM((SB, CB, W), jnp.float32),
        pltpu.VMEM((2, PAIR // 128, CB * 8, 128), jnp.float32),
        pltpu.VMEM((PF // 128, 2 * NV * NV, 128), jnp.float32),
        pltpu.VMEM((PAIR, 4 * PF), jnp.bfloat16),
        pltpu.VMEM((PAIR, 4 * PF), jnp.bfloat16),
        pltpu.VMEM((BLKS, 4 * PF), jnp.float32),
        pltpu.VMEM((BLKS, 4 * PF), jnp.float32),
        pltpu.VMEM((SWEEPS, 2, half, SB, CB, W), jnp.float32),
        pltpu.VMEM((SWEEPS, 2, half - 1, SB, CB, W), jnp.float32),
        pltpu.VMEM((SWEEPS, 2, SB, W), jnp.float32),
        pltpu.VMEM((SWEEPS, 4, 1, W), jnp.float32),
        pltpu.VMEM((SWEEPS, 2, SB, W), jnp.float32),
        pltpu.VMEM((SWEEPS, 2, CB, W), jnp.float32),
        pltpu.VMEM((SWEEPS, 4, 1, W), jnp.float32),
        pltpu.VMEM((SWEEPS, 2, NP, 2 * PF), jnp.float32),
        pltpu.VMEM((SWEEPS, 2, NP, 2 * PF), jnp.float32),
        pltpu.SemaphoreType.DMA((SB + 1,)),
        pltpu.SemaphoreType.DMA((SWEEPS, 2, half, SB)),
        pltpu.SemaphoreType.DMA((SWEEPS, 2, half, SB)),
        pltpu.SemaphoreType.DMA((SWEEPS, 8)),
        pltpu.SemaphoreType.DMA((SWEEPS, 8)),
        pltpu.SemaphoreType.DMA((SWEEPS, 2)),
        pltpu.SemaphoreType.DMA((SWEEPS, 2)),
    ]
    return kernel, scratch


def solution(mesh):
    n_inst, n_span, n_chord = (mesh.shape[a] for a in ("inst", "span", "chord"))

    def per_device(adj_source, adj_start, tiles, tile_cols, inverse_diag, face_src, face_dst, lag_coef):
        _, SB, CB, W = adj_source.shape
        K = tiles.shape[3]
        PF = face_src.shape[1]
        kernel, scratch = make_kernel((SB, CB, W, K, PF), n_inst, n_span, n_chord)
        vmem = pl.BlockSpec(memory_space=pltpu.VMEM)
        out = jax.ShapeDtypeStruct((SB, CB, W), jnp.float32)
        adjoint, residual = pl.pallas_call(
            kernel,
            out_shape=(out, out),
            in_specs=[
                vmem,
                vmem,
                pl.BlockSpec(memory_space=pltpu.SMEM),
                vmem,
                vmem,
                vmem,
                pl.BlockSpec(memory_space=pl.ANY),
                pl.BlockSpec(memory_space=pl.ANY),
            ],
            out_specs=(vmem, vmem),
            scratch_shapes=scratch,
            compiler_params=pltpu.CompilerParams(
                collective_id=0, has_side_effects=True, vmem_limit_bytes=48 * 1024 * 1024
            ),
        )(
            adj_start[0],
            adj_source[0],
            tile_cols.reshape(-1),
            face_src,
            face_dst,
            lag_coef[0],
            tiles.reshape(SB * CB, K, NV, W),
            inverse_diag.reshape(SB * CB, NV, W),
        )
        return adjoint[None], residual[None]

    return jax.shard_map(
        per_device,
        mesh=mesh,
        in_specs=(
            P("inst", "span", "chord", None),
            P("inst", "span", "chord", None),
            P("inst", "span", "chord", None, None, None),
            P("span", "chord", None),
            P("inst", "span", "chord", None, None),
            P(None, ("span", "chord")),
            P(None, ("span", "chord")),
            P("inst", None, ("span", "chord")),
        ),
        out_specs=(P("inst", "span", "chord", None), P("inst", "span", "chord", None)),
        check_vma=False,
    )
```

```python
import math

import jax
import jax.numpy as jnp
from jax import lax
from jax.experimental import pallas as pl
from jax.experimental.pallas import tpu as pltpu
from jax.sharding import PartitionSpec as P

NV = 6
SWEEPS = 2
BLADES = 4
RIGHT, LEFT = 0, 1

rotor_rate = 0.25
spectral_viscosity = 0.03
MESH = pl.DeviceIdType.MESH


def spectral_weight(offset, total):
    m = offset % total
    if m == 0:
        return spectral_viscosity * (total * total + 2) / 12.0
    parity = -1.0 if m % 2 else 1.0
    angle = math.pi * m / total
    first = 0.5 * parity * math.cos(angle) / math.sin(angle)
    second = -0.5 * parity / math.sin(angle) ** 2
    return rotor_rate * first - spectral_viscosity * second


def split3(x):
    high = x.astype(jnp.bfloat16)
    rest = x - high.astype(jnp.float32)
    middle = rest.astype(jnp.bfloat16)
    low = (rest - middle.astype(jnp.float32)).astype(jnp.bfloat16)
    return jnp.concatenate([high, middle, low], axis=0)


def sum3(y):
    n = y.shape[0] // 3
    return (y[2 * n :] + y[n : 2 * n]) + y[:n]


def make_kernel(sizes, n_inst, n_span, n_chord):
    SB, CB, W, K, PF = sizes
    BLK = W // NV
    PAIR = 2 * BLK
    NP = NV // 2
    BLKS = SB * CB
    EXT = CB + 2
    half = n_inst // 2
    lag = n_inst // BLADES

    def kernel(
        x0_ref, source_ref, cols_ref, fsrc_ref, fdst_ref, coef_ref, tiles_hbm, inv_hbm,
        adj_ref, res_ref,
        tiles_ref, inv_ref, x1_ref, xb_ref, base_ref, g_ref, coef32_ref, oh_src, oh_dst, mask_src, mask_dst,
        gat_ref, sum_ref, col_send, corn_send, col_recv, row_recv, corn_recv, pack_send, pack_recv,
        load_sem, gs_sem, gr_sem, hs_sem, hr_sem, ps_sem, pr_sem,
    ):
        t = lax.axis_index("inst")
        sp = lax.axis_index("span")
        ch = lax.axis_index("chord")
        ch_up = lax.rem(ch + 1, n_chord)
        ch_dn = lax.rem(ch + n_chord - 1, n_chord)
        t_up = lax.rem(t + lag, n_inst)
        t_dn = lax.rem(t + n_inst - lag, n_inst)
        has_lo = sp > 0
        has_hi = sp < n_span - 1

        loads = []
        for p in range(SB):
            loads.append(
                pltpu.make_async_copy(
                    tiles_hbm.at[pl.ds(p * CB, CB)], tiles_ref.at[pl.ds(p * CB, CB)], load_sem.at[p]
                )
            )
        inv_load = pltpu.make_async_copy(inv_hbm, inv_ref, load_sem.at[SB])
        for load in loads:
            load.start()
        inv_load.start()

        barrier = pltpu.get_barrier_semaphore()

        def greet(i, s, c):
            pl.semaphore_signal(barrier, inc=1, device_id=(i, s, c), device_id_type=MESH)

        count = 4 + 3 * jnp.where(has_lo, 1, 0) + 3 * jnp.where(has_hi, 1, 0)
        greet(t_up, sp, ch)
        greet(t_dn, sp, ch)
        greet(t, sp, ch_up)
        greet(t, sp, ch_dn)
        if lag != 1:
            count = count + jnp.where(t > 0, 1, 0) + jnp.where(t < n_inst - 1, 1, 0)

            @pl.when(t > 0)
            def _():
                greet(t - 1, sp, ch)

            @pl.when(t < n_inst - 1)
            def _():
                greet(t + 1, sp, ch)

        @pl.when(has_lo)
        def _():
            for c in (ch, ch_up, ch_dn):
                greet(t, sp - 1, c)

        @pl.when(has_hi)
        def _():
            for c in (ch, ch_up, ch_dn):
                greet(t, sp + 1, c)

        pl.semaphore_wait(barrier, count)

        def at(direction):
            return t if direction == RIGHT else n_inst - 1 - t

        def stream(sweep, direction, j, p, src):
            target = t + 1 if direction == RIGHT else t - 1
            return pltpu.make_async_remote_copy(
                src_ref=src,
                dst_ref=gat_ref.at[sweep, direction, j, p],
                send_sem=gs_sem.at[sweep, direction, j, p],
                recv_sem=gr_sem.at[sweep, direction, j, p],
                device_id=(target, sp, ch),
                device_id_type=MESH,
            )

        def weight(direction, hops):
            return spectral_weight(-hops if direction == RIGHT else hops, n_inst)

        def send_own(sweep, p, x_ref):
            for d in (RIGHT, LEFT):

                @pl.when(at(d) < half)
                def _():
                    stream(sweep, d, 0, p, x_ref.at[p]).start()

        def forward(sweep, p):
            for d in (RIGHT, LEFT):
                for j in range(1, half):

                    @pl.when(jnp.logical_and(at(d) >= j, at(d) < half))
                    def _():
                        got = gat_ref.at[sweep, d, j - 1, p]
                        stream(sweep, d, j - 1, p, got).wait_recv()
                        stream(sweep, d, j, p, got).start()

        def collect(sweep, p, x_ref):
            for d in (RIGHT, LEFT):

                @pl.when(at(d) == half)
                def _():
                    for j in range(half):
                        stream(sweep, d, j, p, gat_ref.at[sweep, d, j, p]).wait_recv()
                    for j in range(n_inst - 1 - half):
                        total = weight(d, 1 + j) * x_ref[p]
                        for i in range(half):
                            total = total + weight(d, 2 + j + i) * gat_ref[sweep, d, i, p]
                        sum_ref[sweep, d, j, p] = total
                        stream(sweep, d, j, p, sum_ref.at[sweep, d, j, p]).start()

                for place in range(half + 1, n_inst):

                    @pl.when(at(d) == place)
                    def _():
                        for j in range(n_inst - place):
                            stream(sweep, d, j, p, gat_ref.at[sweep, d, j, p]).wait_recv()
                        for j in range(n_inst - 1 - place):
                            sum_ref[sweep, d, j, p] = gat_ref[sweep, d, j + 1, p] + weight(d, 1 + j) * x_ref[p]
                            stream(sweep, d, j, p, sum_ref.at[sweep, d, j, p]).start()

        def spectral(sweep, p, x_ref):
            res_ref[p] = base_ref[p] - spectral_weight(0, n_inst) * x_ref[p]
            for d in (RIGHT, LEFT):
                for i in range(half):

                    @pl.when(jnp.logical_and(at(d) > i, at(d) <= half))
                    def _():
                        res_ref[p] = res_ref[p] - weight(d, 1 + i) * gat_ref[sweep, d, i, p]

                @pl.when(at(d) > half)
                def _():
                    res_ref[p] = res_ref[p] - gat_ref[sweep, d, 0, p]

        def drain(sweep, p):
            for d in (RIGHT, LEFT):
                for j in range(half):
                    raw = jnp.logical_and(at(d) < half, at(d) >= j)
                    summed = jnp.logical_and(at(d) >= half, at(d) < n_inst - 1 - j)

                    @pl.when(jnp.logical_or(raw, summed))
                    def _():
                        stream(sweep, d, j, p, gat_ref.at[sweep, d, j, p]).wait_send()

        def halo(sweep, place, src, dst, device):
            return pltpu.make_async_remote_copy(
                src_ref=src,
                dst_ref=dst,
                send_sem=hs_sem.at[sweep, place],
                recv_sem=hr_sem.at[sweep, place],
                device_id=device,
                device_id_type=MESH,
            )

        def columns(sweep):
            return [
                halo(sweep, 0, col_send.at[sweep, 0], col_recv.at[sweep, 0], (t, sp, ch_up)),
                halo(sweep, 1, col_send.at[sweep, 1], col_recv.at[sweep, 1], (t, sp, ch_dn)),
            ]

        def upward(sweep, x_ref):
            return [
                halo(sweep, 2, x_ref.at[SB - 1], row_recv.at[sweep, 0], (t, sp + 1, ch)),
                halo(sweep, 4, corn_send.at[sweep, 0], corn_recv.at[sweep, 0], (t, sp + 1, ch_up)),
                halo(sweep, 5, corn_send.at[sweep, 1], corn_recv.at[sweep, 1], (t, sp + 1, ch_dn)),
            ]

        def downward(sweep, x_ref):
            return [
                halo(sweep, 3, x_ref.at[0], row_recv.at[sweep, 1], (t, sp - 1, ch)),
                halo(sweep, 6, corn_send.at[sweep, 2], corn_recv.at[sweep, 2], (t, sp - 1, ch_up)),
                halo(sweep, 7, corn_send.at[sweep, 3], corn_recv.at[sweep, 3], (t, sp - 1, ch_dn)),
            ]

        def send_halos(sweep, x_ref):
            for p in range(SB):
                col_send[sweep, 0, p : p + 1, :] = x_ref[p, CB - 1 : CB, :]
                col_send[sweep, 1, p : p + 1, :] = x_ref[p, 0:1, :]
            corn_send[sweep, 0] = x_ref[SB - 1, CB - 1 : CB, :]
            corn_send[sweep, 1] = x_ref[SB - 1, 0:1, :]
            corn_send[sweep, 2] = x_ref[0, CB - 1 : CB, :]
            corn_send[sweep, 3] = x_ref[0, 0:1, :]
            for copy in columns(sweep):
                copy.start()

            @pl.when(has_hi)
            def _():
                for copy in upward(sweep, x_ref):
                    copy.start()

            @pl.when(has_lo)
            def _():
                for copy in downward(sweep, x_ref):
                    copy.start()

        def put(row, value):
            xb_ref[row] = jnp.broadcast_to(value, (8, W))

        def take_halos(sweep, x_ref):
            for copy in columns(sweep):
                copy.wait_recv()
            for p in range(SB):
                put((p + 1) * EXT, col_recv[sweep, 0, p : p + 1, :])
                put((p + 1) * EXT + CB + 1, col_recv[sweep, 1, p : p + 1, :])

            @pl.when(has_lo)
            def _():
                for copy in upward(sweep, x_ref):
                    copy.wait_recv()
                for q in range(CB):
                    put(q + 1, row_recv[sweep, 0, q : q + 1, :])
                put(0, corn_recv[sweep, 0])
                put(CB + 1, corn_recv[sweep, 1])

            @pl.when(has_hi)
            def _():
                for copy in downward(sweep, x_ref):
                    copy.wait_recv()
                top = (SB + 1) * EXT
                for q in range(CB):
                    put(top + q + 1, row_recv[sweep, 1, q : q + 1, :])
                put(top, corn_recv[sweep, 2])
                put(top + CB + 1, corn_recv[sweep, 3])

        def drain_halos(sweep, x_ref):
            for copy in columns(sweep):
                copy.wait_send()

            @pl.when(has_hi)
            def _():
                for copy in upward(sweep, x_ref):
                    copy.wait_send()

            @pl.when(has_lo)
            def _():
                for copy in downward(sweep, x_ref):
                    copy.wait_send()

        def put_own(p, x_ref):
            for q in range(CB):
                put((p + 1) * EXT + q + 1, x_ref[p, q : q + 1, :])

        def face_tables(faces_ref, onehot, mask):
            faces = jnp.concatenate([faces_ref[s : s + 1, :] for s in (0, 0, 1, 1)], axis=1)
            block = ((faces.astype(jnp.float32) + 0.5) * (1.0 / BLK)).astype(jnp.int32)
            parity = lax.rem(lax.broadcasted_iota(jnp.int32, (1, 4 * PF), 1), 2 * PF) >= PF
            cell = faces - block * BLK + jnp.where(parity, BLK, 0)
            rows = lax.broadcasted_iota(jnp.int32, (BLKS, 4 * PF), 0)
            mask[...] = jnp.where(rows == block, 1.0, 0.0)
            step = 128

            def fill(i, _):
                first = pl.multiple_of(i * step, step)
                lanes = lax.broadcasted_iota(jnp.int32, (step, 4 * PF), 0) + first
                onehot[pl.ds(first, step), :] = jnp.where(lanes == cell, 1.0, 0.0).astype(jnp.bfloat16)
                return 0

            lax.fori_loop(0, PAIR // step, fill, 0)

        def packs(sweep):
            return [
                pltpu.make_async_remote_copy(
                    src_ref=pack_send.at[sweep, side],
                    dst_ref=pack_recv.at[sweep, side],
                    send_sem=ps_sem.at[sweep, side],
                    recv_sem=pr_sem.at[sweep, side],
                    device_id=(target, sp, ch),
                    device_id_type=MESH,
                )
                for side, target in ((0, t_up), (1, t_dn))
            ]

        def send_packs(sweep, x_ref):
            pairs = [x_ref[:, :, m * PAIR : (m + 1) * PAIR].reshape(BLKS, PAIR) for m in range(NP)]
            picked = sum3(
                jnp.dot(
                    split3(jnp.concatenate(pairs, axis=0)), oh_src[...], preferred_element_type=jnp.float32
                )
            )
            for m in range(NP):
                row = jnp.sum(picked[m * BLKS : (m + 1) * BLKS] * mask_src[...], axis=0, keepdims=True)
                for side in (0, 1):
                    pack_send[sweep, side, m : m + 1, :] = row[:, side * 2 * PF : (side + 1) * 2 * PF]
            for copy in packs(sweep):
                copy.start()

        def take_packs(sweep):
            for copy in packs(sweep):
                copy.wait_recv()
            contrib = []
            for side in (0, 1):
                total = jnp.zeros((NV, PF), jnp.float32)
                for w in range(NV):
                    rows = pl.ds(side * NV * NV + w, NV, stride=NV)
                    coupling = jnp.concatenate([coef32_ref[c, rows, :] for c in range(PF // 128)], axis=1)
                    first = (w % 2) * PF
                    total = total + coupling * pack_recv[sweep, side, w // 2 : w // 2 + 1, first : first + PF]
                contrib.append(total)
            spread = []
            for m in range(NP):
                row = jnp.concatenate(
                    [contrib[s][2 * m + odd : 2 * m + odd + 1, :] for s in (0, 1) for odd in (0, 1)], axis=1
                )
                spread.append(mask_dst[...] * row)
            term = sum3(
                lax.dot_general(
                    split3(jnp.concatenate(spread, axis=0)),
                    oh_dst[...],
                    (((1,), (1,)), ((), ())),
                    preferred_element_type=jnp.float32,
                )
            )
            for m in range(NP):
                lanes = slice(m * PAIR, (m + 1) * PAIR)
                base_ref[:, :, lanes] = base_ref[:, :, lanes] - term[m * BLKS : (m + 1) * BLKS].reshape(
                    SB, CB, PAIR
                )

        def fold(product):
            folded = product[:, :PAIR]
            for m in range(1, NP):
                folded = folded + product[:, m * PAIR : (m + 1) * PAIR]
            return folded

        def flat(variable):
            low = lax.broadcasted_iota(jnp.int32, (CB, PAIR), 1) < BLK
            parts = []
            for m in range(NP):
                even, odd = variable(2 * m), variable(2 * m + 1)
                parts.append(
                    jnp.where(low, even, odd) + pltpu.roll(jnp.where(low, odd, even), BLK, axis=1)
                )
            return parts

        def tile_row(p):
            slot = lax.broadcasted_iota(jnp.int32, (K, W), 0)
            for q in range(CB):
                block = p * CB + q
                operand = None
                for k in range(K):
                    code = cols_ref[p, k, q]
                    up = jnp.where(code >= 6, 2, jnp.where(code >= 3, 1, 0))
                    row = (p + up) * EXT + q + code - 3 * up
                    got = xb_ref[row, 0:K, :]
                    operand = got if operand is None else jnp.where(slot == k, got, operand)
                for v in range(NV):
                    folded = fold(tiles_ref[block, v].astype(jnp.float32) * operand)
                    for c in range(PAIR // 128):
                        g_ref[v, c, q * K : (q + 1) * K, :] = folded[:, c * 128 : (c + 1) * 128]

            def variable(v):
                pieces = []
                for c in range(PAIR // 128):
                    rows = [g_ref[v, c, pl.ds(k, CB, stride=K), :] for k in range(K)]
                    pieces.append(sum(rows[1:], rows[0]))
                return jnp.concatenate(pieces, axis=1)

            for m, part in enumerate(flat(variable)):
                lanes = slice(m * PAIR, (m + 1) * PAIR)
                base_ref[p, :, lanes] = source_ref[p, :, lanes] - part

        def update_row(p, x_ref, out_ref):
            residual = res_ref[p]

            def variable(v):
                return fold(inv_ref[p, v].astype(jnp.float32) * residual)

            for m, part in enumerate(flat(variable)):
                lanes = slice(m * PAIR, (m + 1) * PAIR)
                out_ref[p, :, lanes] = x_ref[p, :, lanes] + part

        def loop(body):
            def step(p, _):
                body(p)
                return 0

            lax.fori_loop(0, SB, step, 0)

        send_halos(0, x0_ref)
        loop(lambda p: send_own(0, p, x0_ref))

        @pl.when(jnp.logical_not(has_lo))
        def _():
            for q in range(EXT):
                xb_ref[q] = jnp.zeros((8, W), jnp.float32)

        @pl.when(jnp.logical_not(has_hi))
        def _():
            for q in range(EXT):
                xb_ref[(SB + 1) * EXT + q] = jnp.zeros((8, W), jnp.float32)

        face_tables(fsrc_ref, oh_src, mask_src)
        send_packs(0, x0_ref)
        loop(lambda p: put_own(p, x0_ref))
        face_tables(fdst_ref, oh_dst, mask_dst)
        for c in range(PF // 128):
            coef32_ref[c] = coef_ref[:, c * 128 : (c + 1) * 128].astype(jnp.float32)
        for load in loads:
            load.wait()
        inv_load.wait()
        take_halos(0, x0_ref)

        def first_tiles(p):
            tile_row(p)
            forward(0, p)

        loop(first_tiles)
        take_packs(0)

        def first_update(p):
            collect(0, p, x0_ref)
            spectral(0, p, x0_ref)
            update_row(p, x0_ref, x1_ref)
            send_own(1, p, x1_ref)
            put_own(p, x1_ref)

        loop(first_update)

        send_halos(1, x1_ref)
        send_packs(1, x1_ref)
        take_halos(1, x1_ref)

        def last_tiles(p):
            tile_row(p)
            forward(1, p)

        loop(last_tiles)
        take_packs(1)

        def last_update(p):
            collect(1, p, x1_ref)
            spectral(1, p, x1_ref)
            update_row(p, x1_ref, adj_ref)

        loop(last_update)

        for sweep, x_ref in ((0, x0_ref), (1, x1_ref)):
            loop(lambda p: drain(sweep, p))
            drain_halos(sweep, x_ref)
            for copy in packs(sweep):
                copy.wait_send()

    scratch = [
        pltpu.VMEM((BLKS, NV, K, W), jnp.bfloat16),
        pltpu.VMEM((SB, NV, CB, W), jnp.bfloat16),
        pltpu.VMEM((SB, CB, W), jnp.float32),
        pltpu.VMEM(((SB + 2) * EXT, 8, W), jnp.float32),
        pltpu.VMEM((SB, CB, W), jnp.float32),
        pltpu.VMEM((NV, PAIR // 128, CB * K, 128), jnp.float32),
        pltpu.VMEM((PF // 128, 2 * NV * NV, 128), jnp.float32),
        pltpu.VMEM((PAIR, 4 * PF), jnp.bfloat16),
        pltpu.VMEM((PAIR, 4 * PF), jnp.bfloat16),
        pltpu.VMEM((BLKS, 4 * PF), jnp.float32),
        pltpu.VMEM((BLKS, 4 * PF), jnp.float32),
        pltpu.VMEM((SWEEPS, 2, half, SB, CB, W), jnp.float32),
        pltpu.VMEM((SWEEPS, 2, half - 1, SB, CB, W), jnp.float32),
        pltpu.VMEM((SWEEPS, 2, SB, W), jnp.float32),
        pltpu.VMEM((SWEEPS, 4, 1, W), jnp.float32),
        pltpu.VMEM((SWEEPS, 2, SB, W), jnp.float32),
        pltpu.VMEM((SWEEPS, 2, CB, W), jnp.float32),
        pltpu.VMEM((SWEEPS, 4, 1, W), jnp.float32),
        pltpu.VMEM((SWEEPS, 2, NP, 2 * PF), jnp.float32),
        pltpu.VMEM((SWEEPS, 2, NP, 2 * PF), jnp.float32),
        pltpu.SemaphoreType.DMA((SB + 1,)),
        pltpu.SemaphoreType.DMA((SWEEPS, 2, half, SB)),
        pltpu.SemaphoreType.DMA((SWEEPS, 2, half, SB)),
        pltpu.SemaphoreType.DMA((SWEEPS, 8)),
        pltpu.SemaphoreType.DMA((SWEEPS, 8)),
        pltpu.SemaphoreType.DMA((SWEEPS, 2)),
        pltpu.SemaphoreType.DMA((SWEEPS, 2)),
    ]
    return kernel, scratch


def solution(mesh):
    n_inst, n_span, n_chord = (mesh.shape[a] for a in ("inst", "span", "chord"))

    def per_device(adj_source, adj_start, tiles, tile_cols, inverse_diag, face_src, face_dst, lag_coef):
        _, SB, CB, W = adj_source.shape
        K = tiles.shape[3]
        PF = face_src.shape[1]
        kernel, scratch = make_kernel((SB, CB, W, K, PF), n_inst, n_span, n_chord)
        vmem = pl.BlockSpec(memory_space=pltpu.VMEM)
        out = jax.ShapeDtypeStruct((SB, CB, W), jnp.float32)
        adjoint, residual = pl.pallas_call(
            kernel,
            out_shape=(out, out),
            in_specs=[
                vmem,
                vmem,
                pl.BlockSpec(memory_space=pltpu.SMEM),
                vmem,
                vmem,
                vmem,
                pl.BlockSpec(memory_space=pl.ANY),
                pl.BlockSpec(memory_space=pl.ANY),
            ],
            out_specs=(vmem, vmem),
            scratch_shapes=scratch,
            compiler_params=pltpu.CompilerParams(
                collective_id=0, has_side_effects=True, vmem_limit_bytes=60 * 1024 * 1024
            ),
        )(
            adj_start[0],
            adj_source[0],
            tile_cols.transpose(0, 2, 1),
            face_src,
            face_dst,
            lag_coef[0],
            tiles[0].transpose(0, 1, 3, 2, 4).reshape(SB * CB, NV, K, W),
            inverse_diag[0].transpose(0, 2, 1, 3),
        )
        return adjoint[None], residual[None]

    return jax.shard_map(
        per_device,
        mesh=mesh,
        in_specs=(
            P("inst", "span", "chord", None),
            P("inst", "span", "chord", None),
            P("inst", "span", "chord", None, None, None),
            P("span", "chord", None),
            P("inst", "span", "chord", None, None),
            P(None, ("span", "chord")),
            P(None, ("span", "chord")),
            P("inst", None, ("span", "chord")),
        ),
        out_specs=(P("inst", "span", "chord", None), P("inst", "span", "chord", None)),
        check_vma=False,
    )
```

```python
import math

import jax
import jax.numpy as jnp
from jax import lax
from jax.experimental import pallas as pl
from jax.experimental.pallas import tpu as pltpu
from jax.sharding import PartitionSpec as P

NV = 6
SWEEPS = 2
BLADES = 4
RIGHT, LEFT = 0, 1

rotor_rate = 0.25
spectral_viscosity = 0.03
MESH = pl.DeviceIdType.MESH


def spectral_weight(offset, total):
    m = offset % total
    if m == 0:
        return spectral_viscosity * (total * total + 2) / 12.0
    parity = -1.0 if m % 2 else 1.0
    angle = math.pi * m / total
    first = 0.5 * parity * math.cos(angle) / math.sin(angle)
    second = -0.5 * parity / math.sin(angle) ** 2
    return rotor_rate * first - spectral_viscosity * second


def split(x):
    high = x.astype(jnp.bfloat16)
    low = (x - high.astype(jnp.float32)).astype(jnp.bfloat16)
    return jnp.concatenate([high, low], axis=0)


def join(y):
    n = y.shape[0] // 2
    return y[:n] + y[n:]


def make_kernel(sizes, n_inst, n_span, n_chord):
    SB, CB, W, K, PF = sizes
    BLK = W // NV
    PAIR = 2 * BLK
    NP = NV // 2
    BLKS = SB * CB
    EXT = CB + 2
    half = n_inst // 2
    lag = n_inst // BLADES

    def kernel(
        x0_ref, source_ref, cols_ref, fsrc_ref, fdst_ref, coef_ref, inv_ref, tiles_hbm,
        adj_ref, res_ref,
        tiles_ref, x1_ref, xb_ref, base_ref, g_ref, coef32_ref, oh_src, oh_dst, mask_src, mask_dst,
        gat_ref, sum_ref, col_send, corn_send, col_recv, row_recv, corn_recv, pack_send, pack_recv,
        load_sem, gs_sem, gr_sem, hs_sem, hr_sem, ps_sem, pr_sem,
    ):
        t = lax.axis_index("inst")
        sp = lax.axis_index("span")
        ch = lax.axis_index("chord")
        ch_up = lax.rem(ch + 1, n_chord)
        ch_dn = lax.rem(ch + n_chord - 1, n_chord)
        t_up = lax.rem(t + lag, n_inst)
        t_dn = lax.rem(t + n_inst - lag, n_inst)
        has_lo = sp > 0
        has_hi = sp < n_span - 1

        barrier = pltpu.get_barrier_semaphore()

        def greet(i, s, c):
            pl.semaphore_signal(barrier, inc=1, device_id=(i, s, c), device_id_type=MESH)

        count = 4 + 3 * jnp.where(has_lo, 1, 0) + 3 * jnp.where(has_hi, 1, 0)
        greet(t_up, sp, ch)
        greet(t_dn, sp, ch)
        greet(t, sp, ch_up)
        greet(t, sp, ch_dn)
        if lag != 1:
            count = count + jnp.where(t > 0, 1, 0) + jnp.where(t < n_inst - 1, 1, 0)

            @pl.when(t > 0)
            def _():
                greet(t - 1, sp, ch)

            @pl.when(t < n_inst - 1)
            def _():
                greet(t + 1, sp, ch)

        @pl.when(has_lo)
        def _():
            for c in (ch, ch_up, ch_dn):
                greet(t, sp - 1, c)

        @pl.when(has_hi)
        def _():
            for c in (ch, ch_up, ch_dn):
                greet(t, sp + 1, c)

        loads = []
        for p in range(SB):
            loads.append(
                pltpu.make_async_copy(
                    tiles_hbm.at[pl.ds(p * CB, CB)], tiles_ref.at[pl.ds(p * CB, CB)], load_sem.at[p]
                )
            )
        for load in loads:
            load.start()

        def at(direction):
            return t if direction == RIGHT else n_inst - 1 - t

        def stream(sweep, direction, j, p, src):
            target = t + 1 if direction == RIGHT else t - 1
            return pltpu.make_async_remote_copy(
                src_ref=src,
                dst_ref=gat_ref.at[sweep, direction, j, p],
                send_sem=gs_sem.at[sweep, direction, j, p],
                recv_sem=gr_sem.at[sweep, direction, j, p],
                device_id=(target, sp, ch),
                device_id_type=MESH,
            )

        def weight(direction, hops):
            return spectral_weight(-hops if direction == RIGHT else hops, n_inst)

        def send_own(sweep, p, x_ref):
            for d in (RIGHT, LEFT):

                @pl.when(at(d) < half)
                def _():
                    stream(sweep, d, 0, p, x_ref.at[p]).start()

        def forward(sweep, p):
            for d in (RIGHT, LEFT):
                for j in range(1, half):

                    @pl.when(jnp.logical_and(at(d) >= j, at(d) < half))
                    def _():
                        got = gat_ref.at[sweep, d, j - 1, p]
                        stream(sweep, d, j - 1, p, got).wait_recv()
                        stream(sweep, d, j, p, got).start()

        def collect(sweep, p, x_ref):
            for d in (RIGHT, LEFT):

                @pl.when(at(d) == half)
                def _():
                    for j in range(half):
                        stream(sweep, d, j, p, gat_ref.at[sweep, d, j, p]).wait_recv()
                    for j in range(n_inst - 1 - half):
                        total = weight(d, 1 + j) * x_ref[p]
                        for i in range(half):
                            total = total + weight(d, 2 + j + i) * gat_ref[sweep, d, i, p]
                        sum_ref[sweep, d, j, p] = total
                        stream(sweep, d, j, p, sum_ref.at[sweep, d, j, p]).start()

                for place in range(half + 1, n_inst):

                    @pl.when(at(d) == place)
                    def _():
                        for j in range(n_inst - place):
                            stream(sweep, d, j, p, gat_ref.at[sweep, d, j, p]).wait_recv()
                        for j in range(n_inst - 1 - place):
                            sum_ref[sweep, d, j, p] = gat_ref[sweep, d, j + 1, p] + weight(d, 1 + j) * x_ref[p]
                            stream(sweep, d, j, p, sum_ref.at[sweep, d, j, p]).start()

        def spectral(sweep, p, x_ref):
            res_ref[p] = base_ref[p] - spectral_weight(0, n_inst) * x_ref[p]
            for d in (RIGHT, LEFT):
                for i in range(half):

                    @pl.when(jnp.logical_and(at(d) > i, at(d) <= half))
                    def _():
                        res_ref[p] = res_ref[p] - weight(d, 1 + i) * gat_ref[sweep, d, i, p]

                @pl.when(at(d) > half)
                def _():
                    res_ref[p] = res_ref[p] - gat_ref[sweep, d, 0, p]

        def drain(sweep, p):
            for d in (RIGHT, LEFT):
                for j in range(half):
                    raw = jnp.logical_and(at(d) < half, at(d) >= j)
                    summed = jnp.logical_and(at(d) >= half, at(d) < n_inst - 1 - j)

                    @pl.when(jnp.logical_or(raw, summed))
                    def _():
                        stream(sweep, d, j, p, gat_ref.at[sweep, d, j, p]).wait_send()

        def halo(sweep, place, src, dst, device):
            return pltpu.make_async_remote_copy(
                src_ref=src,
                dst_ref=dst,
                send_sem=hs_sem.at[sweep, place],
                recv_sem=hr_sem.at[sweep, place],
                device_id=device,
                device_id_type=MESH,
            )

        def columns(sweep):
            return [
                halo(sweep, 0, col_send.at[sweep, 0], col_recv.at[sweep, 0], (t, sp, ch_up)),
                halo(sweep, 1, col_send.at[sweep, 1], col_recv.at[sweep, 1], (t, sp, ch_dn)),
            ]

        def upward(sweep, x_ref):
            return [
                halo(sweep, 2, x_ref.at[SB - 1], row_recv.at[sweep, 0], (t, sp + 1, ch)),
                halo(sweep, 4, corn_send.at[sweep, 0], corn_recv.at[sweep, 0], (t, sp + 1, ch_up)),
                halo(sweep, 5, corn_send.at[sweep, 1], corn_recv.at[sweep, 1], (t, sp + 1, ch_dn)),
            ]

        def downward(sweep, x_ref):
            return [
                halo(sweep, 3, x_ref.at[0], row_recv.at[sweep, 1], (t, sp - 1, ch)),
                halo(sweep, 6, corn_send.at[sweep, 2], corn_recv.at[sweep, 2], (t, sp - 1, ch_up)),
                halo(sweep, 7, corn_send.at[sweep, 3], corn_recv.at[sweep, 3], (t, sp - 1, ch_dn)),
            ]

        def stage_columns(sweep, p, x_ref):
            col_send[sweep, 0, p] = x_ref[p, CB - 1 : CB, :]
            col_send[sweep, 1, p] = x_ref[p, 0:1, :]

        def send_columns(sweep):
            for copy in columns(sweep):
                copy.start()

        def send_up(sweep, x_ref):
            @pl.when(has_hi)
            def _():
                corn_send[sweep, 0] = x_ref[SB - 1, CB - 1 : CB, :]
                corn_send[sweep, 1] = x_ref[SB - 1, 0:1, :]
                for copy in upward(sweep, x_ref):
                    copy.start()

        def send_down(sweep, x_ref):
            @pl.when(has_lo)
            def _():
                corn_send[sweep, 2] = x_ref[0, CB - 1 : CB, :]
                corn_send[sweep, 3] = x_ref[0, 0:1, :]
                for copy in downward(sweep, x_ref):
                    copy.start()

        def put(row, value):
            xb_ref[row] = jnp.broadcast_to(value, (8, W))

        def take_halos(sweep, x_ref):
            for copy in columns(sweep):
                copy.wait_recv()
            for p in range(SB):
                put((p + 1) * EXT, col_recv[sweep, 0, p])
                put((p + 1) * EXT + CB + 1, col_recv[sweep, 1, p])

            @pl.when(has_lo)
            def _():
                for copy in upward(sweep, x_ref):
                    copy.wait_recv()
                for q in range(CB):
                    put(q + 1, row_recv[sweep, 0, q : q + 1, :])
                put(0, corn_recv[sweep, 0])
                put(CB + 1, corn_recv[sweep, 1])

            @pl.when(has_hi)
            def _():
                for copy in downward(sweep, x_ref):
                    copy.wait_recv()
                top = (SB + 1) * EXT
                for q in range(CB):
                    put(top + q + 1, row_recv[sweep, 1, q : q + 1, :])
                put(top, corn_recv[sweep, 2])
                put(top + CB + 1, corn_recv[sweep, 3])

        def drain_halos(sweep, x_ref):
            for copy in columns(sweep):
                copy.wait_send()

            @pl.when(has_hi)
            def _():
                for copy in upward(sweep, x_ref):
                    copy.wait_send()

            @pl.when(has_lo)
            def _():
                for copy in downward(sweep, x_ref):
                    copy.wait_send()

        def put_own(p, x_ref):
            for q in range(CB):
                put((p + 1) * EXT + q + 1, x_ref[p, q : q + 1, :])

        def face_cells(faces_ref, mask):
            faces = jnp.concatenate([faces_ref[s : s + 1, :] for s in (0, 0, 1, 1)], axis=1)
            block = ((faces.astype(jnp.float32) + 0.5) * (1.0 / BLK)).astype(jnp.int32)
            parity = lax.rem(lax.broadcasted_iota(jnp.int32, (1, 4 * PF), 1), 2 * PF) >= PF
            rows = lax.broadcasted_iota(jnp.int32, (BLKS, 4 * PF), 0)
            mask[...] = jnp.where(rows == block, 1.0, 0.0)
            return faces - block * BLK + jnp.where(parity, BLK, 0)

        def source_table():
            cell = face_cells(fsrc_ref, mask_src)

            def fill(i, _):
                first = pl.multiple_of(i * 128, 128)
                lanes = lax.broadcasted_iota(jnp.int32, (128, 4 * PF), 0) + first
                oh_src[pl.ds(first, 128), :] = jnp.where(lanes == cell, 1.0, 0.0).astype(jnp.bfloat16)
                return 0

            lax.fori_loop(0, PAIR // 128, fill, 0)

        def target_table():
            cell = face_cells(fdst_ref, mask_dst).astype(jnp.float32)
            lanes = lax.broadcasted_iota(jnp.int32, (128, 128), 1).astype(jnp.float32)
            for j in range(0, 4 * PF, 128):
                column = jnp.broadcast_to(cell[:, j : j + 128], (128, 128)).T
                for c in range(0, PAIR, 128):
                    oh_dst[j : j + 128, c : c + 128] = jnp.where(lanes + float(c) == column, 1.0, 0.0).astype(
                        jnp.bfloat16
                    )

        def packs(sweep):
            return [
                pltpu.make_async_remote_copy(
                    src_ref=pack_send.at[sweep, side],
                    dst_ref=pack_recv.at[sweep, side],
                    send_sem=ps_sem.at[sweep, side],
                    recv_sem=pr_sem.at[sweep, side],
                    device_id=(target, sp, ch),
                    device_id_type=MESH,
                )
                for side, target in ((0, t_up), (1, t_dn))
            ]

        def send_packs(sweep, x_ref):
            pairs = [x_ref[:, :, m * PAIR : (m + 1) * PAIR].reshape(BLKS, PAIR) for m in range(NP)]
            picked = join(
                jnp.dot(
                    split(jnp.concatenate(pairs, axis=0)), oh_src[...], preferred_element_type=jnp.float32
                )
            )
            for m in range(NP):
                row = jnp.sum(picked[m * BLKS : (m + 1) * BLKS] * mask_src[...], axis=0, keepdims=True)
                for side in (0, 1):
                    pack_send[sweep, side, m : m + 1, :] = row[:, side * 2 * PF : (side + 1) * 2 * PF]
            for copy in packs(sweep):
                copy.start()

        def take_packs(sweep):
            for copy in packs(sweep):
                copy.wait_recv()
            contrib = []
            for side in (0, 1):
                total = jnp.zeros((NV, PF), jnp.float32)
                for w in range(NV):
                    rows = pl.ds(side * NV * NV + w, NV, stride=NV)
                    coupling = jnp.concatenate([coef32_ref[c, rows, :] for c in range(PF // 128)], axis=1)
                    first = (w % 2) * PF
                    total = total + coupling * pack_recv[sweep, side, w // 2 : w // 2 + 1, first : first + PF]
                contrib.append(total)
            spread = []
            for m in range(NP):
                row = jnp.concatenate(
                    [contrib[s][2 * m + odd : 2 * m + odd + 1, :] for s in (0, 1) for odd in (0, 1)], axis=1
                )
                spread.append(mask_dst[...] * row)
            term = join(
                jnp.dot(
                    split(jnp.concatenate(spread, axis=0)), oh_dst[...], preferred_element_type=jnp.float32
                )
            )
            for m in range(NP):
                lanes = slice(m * PAIR, (m + 1) * PAIR)
                base_ref[:, :, lanes] = base_ref[:, :, lanes] - term[m * BLKS : (m + 1) * BLKS].reshape(
                    SB, CB, PAIR
                )

        def fold(product):
            folded = product[:, :PAIR]
            for m in range(1, NP):
                folded = folded + product[:, m * PAIR : (m + 1) * PAIR]
            return folded

        def flat(variable):
            low = lax.broadcasted_iota(jnp.int32, (CB, PAIR), 1) < BLK
            parts = []
            for m in range(NP):
                even, odd = variable(2 * m), variable(2 * m + 1)
                parts.append(
                    jnp.where(low, even, odd) + pltpu.roll(jnp.where(low, odd, even), BLK, axis=1)
                )
            return parts

        def tile_blocks(p, blocks):
            slot = lax.broadcasted_iota(jnp.int32, (K, W), 0)
            for q in blocks:
                block = p * CB + q
                operand = None
                for k in range(K):
                    code = cols_ref[p, k, q]
                    up = jnp.where(code >= 6, 2, jnp.where(code >= 3, 1, 0))
                    row = (p + up) * EXT + q + code - 3 * up
                    got = xb_ref[row, 0:K, :]
                    operand = got if operand is None else jnp.where(slot == k, got, operand)
                for v in range(NV):
                    folded = fold(tiles_ref[block, v].astype(jnp.float32) * operand)
                    for c in range(PAIR // 128):
                        g_ref[p, v, c, q * K : (q + 1) * K, :] = folded[:, c * 128 : (c + 1) * 128]

        def finish_tiles(p):
            def variable(v):
                pieces = []
                for c in range(PAIR // 128):
                    rows = [g_ref[p, v, c, pl.ds(k, CB, stride=K), :] for k in range(K)]
                    pieces.append(sum(rows[1:], rows[0]))
                return jnp.concatenate(pieces, axis=1)

            for m, part in enumerate(flat(variable)):
                lanes = slice(m * PAIR, (m + 1) * PAIR)
                base_ref[p, :, lanes] = source_ref[p, :, lanes] - part

        def update_row(p, x_ref, out_ref):
            residual = res_ref[p]

            def variable(v):
                return fold(inv_ref[p, v].astype(jnp.float32) * residual)

            for m, part in enumerate(flat(variable)):
                lanes = slice(m * PAIR, (m + 1) * PAIR)
                out_ref[p, :, lanes] = x_ref[p, :, lanes] + part

        def loop(body, first=0, last=SB):
            def step(p, _):
                body(p)
                return 0

            lax.fori_loop(first, last, step, 0)

        inner = range(1, CB - 1)

        def inner_tiles(p):
            tile_blocks(p, inner)

        def outer_tiles(sweep):
            def end_row(i):
                p = i * (SB - 1)
                tile_blocks(p, range(CB))
                finish_tiles(p)
                forward(sweep, i)

            def middle_row(p):
                tile_blocks(p, (0, CB - 1))
                finish_tiles(p)
                forward(sweep, p + 1)

            loop(end_row, 0, 2)
            loop(middle_row, 1, SB - 1)

        loop(lambda p: stage_columns(0, p, x0_ref))
        pl.semaphore_wait(barrier, count)
        loop(lambda p: send_own(0, p, x0_ref), 0, 1)
        send_columns(0)
        send_up(0, x0_ref)
        send_down(0, x0_ref)
        loop(lambda p: send_own(0, p, x0_ref), 1, SB)

        @pl.when(jnp.logical_not(has_lo))
        def _():
            for q in range(EXT):
                xb_ref[q] = jnp.zeros((8, W), jnp.float32)

        @pl.when(jnp.logical_not(has_hi))
        def _():
            for q in range(EXT):
                xb_ref[(SB + 1) * EXT + q] = jnp.zeros((8, W), jnp.float32)

        source_table()
        send_packs(0, x0_ref)
        loop(lambda p: put_own(p, x0_ref))
        for load in loads:
            load.wait()
        loop(inner_tiles, 1, SB - 1)
        take_halos(0, x0_ref)
        outer_tiles(0)
        target_table()
        for c in range(PF // 128):
            coef32_ref[c] = coef_ref[:, c * 128 : (c + 1) * 128].astype(jnp.float32)
        take_packs(0)

        def first_update(p):
            collect(0, p, x0_ref)
            spectral(0, p, x0_ref)
            update_row(p, x0_ref, x1_ref)
            send_own(1, p, x1_ref)
            stage_columns(1, p, x1_ref)

            @pl.when(p == 0)
            def _():
                send_down(1, x1_ref)

            @pl.when(p == SB - 1)
            def _():
                send_columns(1)
                send_up(1, x1_ref)

            put_own(p, x1_ref)

        loop(first_update)

        send_packs(1, x1_ref)
        loop(inner_tiles, 1, SB - 1)
        take_halos(1, x1_ref)
        outer_tiles(1)
        take_packs(1)

        def last_update(p):
            collect(1, p, x1_ref)
            spectral(1, p, x1_ref)
            update_row(p, x1_ref, adj_ref)

        loop(last_update)

        for sweep, x_ref in ((0, x0_ref), (1, x1_ref)):
            loop(lambda p: drain(sweep, p))
            drain_halos(sweep, x_ref)
            for copy in packs(sweep):
                copy.wait_send()

    scratch = [
        pltpu.VMEM((BLKS, NV, K, W), jnp.bfloat16),
        pltpu.VMEM((SB, CB, W), jnp.float32),
        pltpu.VMEM(((SB + 2) * EXT, 8, W), jnp.float32),
        pltpu.VMEM((SB, CB, W), jnp.float32),
        pltpu.VMEM((SB, NV, PAIR // 128, CB * K, 128), jnp.float32),
        pltpu.VMEM((PF // 128, 2 * NV * NV, 128), jnp.float32),
        pltpu.VMEM((PAIR, 4 * PF), jnp.bfloat16),
        pltpu.VMEM((4 * PF, PAIR), jnp.bfloat16),
        pltpu.VMEM((BLKS, 4 * PF), jnp.float32),
        pltpu.VMEM((BLKS, 4 * PF), jnp.float32),
        pltpu.VMEM((SWEEPS, 2, half, SB, CB, W), jnp.float32),
        pltpu.VMEM((SWEEPS, 2, half - 1, SB, CB, W), jnp.float32),
        pltpu.VMEM((SWEEPS, 2, SB, 1, W), jnp.float32),
        pltpu.VMEM((SWEEPS, 4, 1, W), jnp.float32),
        pltpu.VMEM((SWEEPS, 2, SB, 1, W), jnp.float32),
        pltpu.VMEM((SWEEPS, 2, CB, W), jnp.float32),
        pltpu.VMEM((SWEEPS, 4, 1, W), jnp.float32),
        pltpu.VMEM((SWEEPS, 2, NP, 2 * PF), jnp.float32),
        pltpu.VMEM((SWEEPS, 2, NP, 2 * PF), jnp.float32),
        pltpu.SemaphoreType.DMA((SB,)),
        pltpu.SemaphoreType.DMA((SWEEPS, 2, half, SB)),
        pltpu.SemaphoreType.DMA((SWEEPS, 2, half, SB)),
        pltpu.SemaphoreType.DMA((SWEEPS, 8)),
        pltpu.SemaphoreType.DMA((SWEEPS, 8)),
        pltpu.SemaphoreType.DMA((SWEEPS, 2)),
        pltpu.SemaphoreType.DMA((SWEEPS, 2)),
    ]
    return kernel, scratch


def solution(mesh):
    n_inst, n_span, n_chord = (mesh.shape[a] for a in ("inst", "span", "chord"))

    def per_device(adj_source, adj_start, tiles, tile_cols, inverse_diag, face_src, face_dst, lag_coef):
        _, SB, CB, W = adj_source.shape
        K = tiles.shape[3]
        PF = face_src.shape[1]
        kernel, scratch = make_kernel((SB, CB, W, K, PF), n_inst, n_span, n_chord)
        vmem = pl.BlockSpec(memory_space=pltpu.VMEM)
        out = jax.ShapeDtypeStruct((SB, CB, W), jnp.float32)
        adjoint, residual = pl.pallas_call(
            kernel,
            out_shape=(out, out),
            in_specs=[
                vmem,
                vmem,
                pl.BlockSpec(memory_space=pltpu.SMEM),
                vmem,
                vmem,
                vmem,
                vmem,
                pl.BlockSpec(memory_space=pl.ANY),
            ],
            out_specs=(vmem, vmem),
            scratch_shapes=scratch,
            compiler_params=pltpu.CompilerParams(
                collective_id=0, has_side_effects=True, vmem_limit_bytes=52 * 1024 * 1024
            ),
        )(
            adj_start[0],
            adj_source[0],
            tile_cols.transpose(0, 2, 1),
            face_src,
            face_dst,
            lag_coef[0],
            inverse_diag[0].transpose(0, 2, 1, 3),
            tiles[0].transpose(0, 1, 3, 2, 4).reshape(SB * CB, NV, K, W),
        )
        return adjoint[None], residual[None]

    return jax.shard_map(
        per_device,
        mesh=mesh,
        in_specs=(
            P("inst", "span", "chord", None),
            P("inst", "span", "chord", None),
            P("inst", "span", "chord", None, None, None),
            P("span", "chord", None),
            P("inst", "span", "chord", None, None),
            P(None, ("span", "chord")),
            P(None, ("span", "chord")),
            P("inst", None, ("span", "chord")),
        ),
        out_specs=(P("inst", "span", "chord", None), P("inst", "span", "chord", None)),
        check_vma=False,
    )
```
